32 devices in a mesh: occ: 2 (over x), vw: 8 (over z, y), vn: 2 (over core).
Axes of the slice: x: 2, y: 2, z: 4, core: 2. Of those that a mesh axis runs over, the one named last changes fastest.
Arguments:
- slabs: bfloat16 [2, 5120, 10240], P('occ', 'vw', 'vn'), may hold values from -0.125 to 0.125
- pair_list: int32 [1, 2], replicated, may hold values from 0 to 1
- occ_energy: float32 [2], replicated, may hold values from -1.2 to -0.4
- virt_energy: float32 [5120], replicated, may hold values from 0.2 to 2.5
Outputs:
- density: float32 [5120, 5120], P('vw', ('occ', 'vn'))
The draws below stay inside these ranges and needn't reach their ends.
Inputs may be any that keep to these rules, and one draw needn't show every extreme that they name: `pair_list`: entries are orbital indices of the window; both entries of a pair may be equal.
All inputs are finite; a program needn't handle non-finite values.
Results may differ from the reference program's by a relative error of at most 0.0035.
Values may be sent and summed in bfloat16 or wider, within the bound.
No kernel may reach another device: no remote copies, remote signals or barrier semaphores. Data moves between devices by JAX's collectives and lax.ppermute only.
A program may use at most 128 MiB of HBM per device.

```python
import jax
import jax.numpy as jnp
from jax import lax

V = 5120
Q = 10240
NPAIRS = 1
NOCC = 2


def steps_of(rng, extent, shards, smallest, high):
    def one(position, parts):
        heights = jax.random.uniform(jax.random.fold_in(jax.random.fold_in(rng, 6), position), (parts,), jnp.float32, smallest / len(shards), high / len(shards))
        return jnp.repeat(jnp.exp(heights), extent[position] // parts).reshape((-1,) + (1,) * (len(extent) - position - 1))

    loudness = one(*shards[0])
    for cut in shards[1:]:
        loudness = loudness * one(*cut)
    return loudness


def bell_draw(rng, extent, spread, reach, split=(), dtype=jnp.bfloat16):
    gain = steps_of(rng, extent, split, -0.22, 0.18) if split else 1.0
    result = jax.random.normal(rng, extent, jnp.float32) * spread * gain
    return jnp.minimum(jnp.maximum(result, -reach), reach).astype(dtype)


def setup_inputs(seed: int = 0) -> dict:
    key_of = jax.random.split(jax.random.key(seed), 5)
    slabs = bell_draw(key_of[0], (NOCC, V, Q), (1.8 * (Q * V) ** -0.25), 0.125, ((0, 2), (1, 8), (2, 2)))
    pair_list = jax.random.randint(key_of[1], (NPAIRS, 2), 0, NOCC).astype(jnp.int32)
    occ_energy = jnp.clip(jax.random.uniform(key_of[2], (NOCC,), jnp.float32, -1.2, -0.4), -1.2, -0.4)
    virt_energy = jnp.clip(jax.random.uniform(key_of[3], (V,), jnp.float32, 0.2, 2.5), 0.2, 2.5)
    return {"slabs": slabs, "pair_list": pair_list, "occ_energy": occ_energy, "virt_energy": virt_energy}


def reference(slabs, pair_list, occ_energy, virt_energy):
    density = jnp.zeros((V, V), jnp.float32)
    for index in range(NPAIRS):
        first = pair_list[index, 0]
        second = pair_list[index, 1]
        row_slab = lax.dynamic_index_in_dim(slabs, first, 0, keepdims=False)
        col_slab = lax.dynamic_index_in_dim(slabs, second, 0, keepdims=False)
        integrals = jnp.dot(row_slab, col_slab.T, preferred_element_type=jnp.float32)
        denom = occ_energy[first] + occ_energy[second] - virt_energy[:, None] - virt_energy[None, :]
        amplitudes = (integrals / denom).astype(jnp.bfloat16)
        density = density + jnp.dot(amplitudes, amplitudes.T, preferred_element_type=jnp.float32)
    return density
```

```python
import math

import jax
import jax.numpy as jnp
from jax import lax
from jax.sharding import PartitionSpec as P

CHUNKS = 2


def contract_rows(left, piece):
    return lax.dot_general(
        left, piece, (((1,), (1,)), ((), ())), preferred_element_type=jnp.float32
    )


def contract_first(left, right):
    return lax.dot_general(
        left, right, (((0,), (0,)), ((), ())), preferred_element_type=jnp.float32
    )


def pick(items, index):
    chosen = items[0]
    for position in range(1, len(items)):
        chosen = jnp.where(index == position, items[position], chosen)
    return chosen


def cuts(extent, parts):
    unit = 16 if extent % 16 == 0 and extent // 16 >= parts else 1
    marks = [extent // unit * part // parts * unit for part in range(parts + 1)]
    return [(low, high) for low, high in zip(marks, marks[1:]) if high > low]


def whole_rows(slabs, pair_list, occ_energy, virt_energy):
    n_vw = lax.axis_size("vw")
    n_occ = lax.axis_size("occ")
    n_vn = lax.axis_size("vn")
    tile_rows = slabs.shape[1]
    sub_rows = tile_rows // n_occ
    my_occ = lax.axis_index("occ")
    my_vw = lax.axis_index("vw")
    my_vn = lax.axis_index("vn")
    row_energy = lax.dynamic_slice_in_dim(virt_energy, my_vw * tile_rows, tile_rows)
    energy_grid = virt_energy.reshape(n_vw, n_occ, sub_rows)
    col_energy = lax.dynamic_index_in_dim(energy_grid, my_occ, 1, keepdims=False).reshape(
        n_vw * sub_rows
    )
    share = n_vw * sub_rows // n_vn
    col_share = lax.dynamic_slice_in_dim(col_energy, my_vn * share, share)
    pieces = lax.all_to_all(slabs, "occ", split_axis=1, concat_axis=0, tiled=True)
    density = 0.0
    for index in range(pair_list.shape[0]):
        first = pair_list[index, 0]
        second = pair_list[index, 1]
        first_piece = lax.dynamic_index_in_dim(pieces, first, 0, keepdims=False)
        row_tile = lax.all_gather(first_piece, "occ", axis=0, tiled=True)
        col_piece = lax.dynamic_index_in_dim(pieces, second, 0, keepdims=False)
        integrals = contract_rows(row_tile, lax.all_gather(col_piece, "vw", axis=0, tiled=True))
        summed = lax.psum(integrals, "vn")
        mine = lax.dynamic_slice_in_dim(summed, my_vn * share, share, 1)
        denom = occ_energy[first] + occ_energy[second] - row_energy[:, None] - col_share[None, :]
        amplitude = (mine / denom).astype(jnp.bfloat16)
        density += contract_rows(amplitude, lax.all_gather(amplitude, "vw", axis=0, tiled=True))
    return lax.psum_scatter(density, ("occ", "vn"), scatter_dimension=1, tiled=True)


def grid_blocks(slabs, pair_list, occ_energy, virt_energy):
    n_vw, n_occ, n_vn = (lax.axis_size(name) for name in ("vw", "occ", "vn"))
    side = math.isqrt(n_occ * n_vn)
    depth = n_vw // (side * side)
    group = side // n_vn
    held, tile, k_dev = slabs.shape
    sub = tile // n_occ
    k_part = k_dev // n_occ
    x, w, v = (lax.axis_index(name) for name in ("occ", "vw", "vn"))
    r, s, y = w // (side * depth), w // depth % side, w % depth

    def at(row, col, deep):
        return (row % side * side + col % side) * depth + deep % depth

    places = [(a, b, c) for a in range(side) for b in range(side) for c in range(depth)]

    def send_vw(array, target):
        pairs = [(at(*place), at(*target(*place))) for place in places]
        if all(source == goal for source, goal in pairs):
            return array
        return lax.ppermute(array, "vw", pairs)

    def send_on(array, axis, extent, step):
        return lax.ppermute(array, axis, [(a, (a + step) % extent) for a in range(extent)])

    rows_by_sub = slabs.reshape(held, n_occ, sub, k_dev)
    energy = virt_energy.reshape(n_vw, n_occ, sub)
    chunks = cuts(sub, CHUNKS)

    shares = []
    for low, high in chunks:
        rows = rows_by_sub[:, :, low:high]
        parts = [
            lax.dynamic_slice_in_dim(rows, (x + step) % n_occ * k_part, k_part, 3)
            for step in range(n_occ)
        ]
        shares.append(
            [parts[0]] + [send_on(parts[step], "occ", n_occ, step) for step in range(1, n_occ)]
        )

    def orbital_rows(share, orbital):
        mine = [lax.dynamic_index_in_dim(part, orbital % held, 0, keepdims=False) for part in share]
        return pick(mine, (x - orbital // held) % n_occ)

    total = 0.0
    for index in range(pair_list.shape[0]):
        first, second = pair_list[index, 0], pair_list[index, 1]
        row_shares = [orbital_rows(share, first) for share in shares]
        col_shares = [
            jnp.roll(orbital_rows(share, second), -x, 0) for share in shares
        ]
        row_parts = [
            [part] + [send_vw(part, lambda a, b, c, d=d: (a, b - d, c)) for d in range(1, side)]
            for part in row_shares
        ]
        tiles = [
            jnp.concatenate([part[d] for part in row_parts], 1).reshape(tile, k_part)
            for d in range(side)
        ]
        row_sets = []
        for step in range(n_vn):
            core = (v + step) % n_vn
            row_sets.append(
                jnp.concatenate(
                    [pick(tiles, (q * n_vn + core - s) % side) for q in range(group)], 0
                )
            )
        row_index = [at(r, q * n_vn + v, y) for q in range(group)]
        row_energy = jnp.concatenate(
            [lax.dynamic_index_in_dim(energy, i, 0, keepdims=False).reshape(tile) for i in row_index]
        )
        pair_energy = occ_energy[first] + occ_energy[second]

        amplitude = []
        for d in range(side):
            amplitude.append([])
            for part, (low, high) in zip(col_shares, chunks):
                arrived = send_vw(part, lambda a, b, c, d=d: (b - d, a, c))
                columns = [arrived] + [
                    send_vw(arrived, lambda a, b, c, l=l: (a, b, c - l)) for l in range(1, depth)
                ]
                size = depth * (high - low)
                sums = []
                for step in range(n_occ):
                    these = jnp.stack([col[step] for col in columns]).reshape(size, k_part)
                    sums.append([contract_rows(these, rows) for rows in row_sets])
                done = []
                for partial in sums:
                    kept = partial[0]
                    for step in range(1, n_vn):
                        kept = kept + send_on(partial[step], "vn", n_vn, step)
                    done.append(kept)
                integrals = done[0]
                for step in range(1, n_occ):
                    integrals = integrals + send_on(done[step], "occ", n_occ, step)
                col_energy = jnp.concatenate(
                    [
                        lax.dynamic_slice(
                            energy, (at(s, r + d, y + l), x, low), (1, 1, high - low)
                        ).reshape(high - low)
                        for l in range(depth)
                    ]
                )
                denom = pair_energy - row_energy[None, :] - col_energy[:, None]
                block = (integrals / denom).astype(jnp.bfloat16)
                amplitude[d].append(block.reshape(depth, high - low, block.shape[1]))

        def in_order(blocks, row, deep):
            ordered = []
            for a in range(side):
                by_tile = [
                    pick([blocks[d][h] for d in range(side)], (a - row) % side)
                    for h in range(len(chunks))
                ]
                for b in range(depth):
                    ordered += [
                        pick([part[l] for l in range(depth)], (b - deep) % depth)
                        for part in by_tile
                    ]
            return jnp.concatenate(ordered, 0)

        gathered = {}
        for a in range(side):
            for c in range(depth):
                if a == 0 and c == 0:
                    gathered[a, c] = in_order(amplitude, r, y)
                elif c == 0:
                    gathered[a, c] = send_vw(
                        gathered[0, 0], lambda i, j, k, a=a: (i - a, j, k)
                    )
                else:
                    gathered[a, c] = send_vw(
                        gathered[a, 0], lambda i, j, k, c=c: (i, j, k - c)
                    )
        cores = [gathered[0, 0]] + [
            send_on(gathered[0, 0], "vn", n_vn, n_vn - step) for step in range(1, n_vn)
        ]
        count = gathered[0, 0].shape[0]
        by_s = [
            pick([core.reshape(count, group, tile)[:, q] for core in cores], (b - v) % n_vn)
            for q in range(group)
            for b in range(n_vn)
        ]
        left = [pick(by_s, (s + d) % side) for d in range(side)]

        def right(step, deep):
            goal = (x + step) % n_occ
            split = [gathered[a, deep].reshape(count, group, tile) for a in range(side)]
            options = [split[(a)][:, q] for a in range(side) for q in range(group)]
            return pick(options, (goal // group - r) % side * group + goal % group)

        parts = []
        for deep in range(depth):
            rights = [right(step, deep) for step in range(n_occ)]
            terms = [[contract_first(rows, cols) for cols in rights] for rows in left]
            if deep % 2 == 0:
                by_row = []
                for row in terms:
                    kept = row[0]
                    for step in range(1, n_occ):
                        kept = kept + send_on(
                            row[step].astype(jnp.bfloat16), "occ", n_occ, step
                        ).astype(jnp.float32)
                    by_row.append(kept)
                kept = by_row[0]
                for d in range(1, side):
                    kept = kept + send_vw(
                        by_row[d].astype(jnp.bfloat16), lambda i, j, k, d=d: (i, j + d, k)
                    ).astype(jnp.float32)
            else:
                by_col = []
                for step in range(n_occ):
                    kept = terms[0][step]
                    for d in range(1, side):
                        kept = kept + send_vw(
                            terms[d][step].astype(jnp.bfloat16),
                            lambda i, j, k, d=d: (i, j + d, k),
                        ).astype(jnp.float32)
                    by_col.append(kept)
                kept = by_col[0]
                for step in range(1, n_occ):
                    kept = kept + send_on(
                        by_col[step].astype(jnp.bfloat16), "occ", n_occ, step
                    ).astype(jnp.float32)
            parts.append(kept)
        ordered = [pick(parts, (c - y) % depth) for c in range(depth)]
        total = total + jnp.concatenate(ordered, 1)
    return total


def solution(mesh):
    in_specs = (P("occ", "vw", "vn"), P(), P(), P())
    out_specs = P("vw", ("occ", "vn"))
    n_occ, n_vw, n_vn = (mesh.shape[name] for name in ("occ", "vw", "vn"))
    side = math.isqrt(n_occ * n_vn)
    fits = side * side == n_occ * n_vn and n_vw % (side * side) == 0 and side % n_vn == 0
    return jax.shard_map(
        grid_blocks if fits else whole_rows,
        mesh=mesh,
        in_specs=in_specs,
        out_specs=out_specs,
        check_vma=False,
    )
```

```python
import math

import jax
import jax.numpy as jnp
from jax import lax
from jax.sharding import PartitionSpec as P

SHARES = (1, 1, 1, 1)
FIRST_SETS = (4,)
OTHER_SETS = (2, 3, 4)
HALVES = (3, 2)
TERM = jnp.bfloat16
LAG_X = 9
LAG_Z = 1
LAG_Y = 1


def contract_rows(left, piece):
    return lax.dot_general(
        left, piece, (((1,), (1,)), ((), ())), preferred_element_type=jnp.float32
    )


def contract_first(left, right):
    return lax.dot_general(
        left, right, (((0,), (0,)), ((), ())), preferred_element_type=jnp.float32
    )


def pick(items, index):
    chosen = items[0]
    for position in range(1, len(items)):
        chosen = jnp.where(index == position, items[position], chosen)
    return chosen


def cuts(extent, shares, unit=16):
    whole = sum(shares)
    if extent % unit or extent // unit < whole:
        unit = 1
    marks = [extent // unit * sum(shares[:part]) // whole * unit for part in range(len(shares) + 1)]
    return [(low, high) for low, high in zip(marks, marks[1:]) if high > low]


def ends_of(sets, count):
    return sorted({min(end, count) for end in sets} | {count})


class Lane:
    def __init__(self, lag):
        self.arrived = []
        self.lag = lag

    @staticmethod
    def send(lanes, array, move):
        waits = [lane.arrived[-lane.lag] for lane in lanes if len(lane.arrived) >= lane.lag]
        if waits:
            array, *_ = lax.optimization_barrier((array, *waits))
        result = move(array)
        for lane in lanes:
            lane.arrived.append(result)
        return result


def whole_rows(slabs, pair_list, occ_energy, virt_energy):
    n_vw = lax.axis_size("vw")
    n_occ = lax.axis_size("occ")
    n_vn = lax.axis_size("vn")
    tile_rows = slabs.shape[1]
    sub_rows = tile_rows // n_occ
    my_occ = lax.axis_index("occ")
    my_vw = lax.axis_index("vw")
    my_vn = lax.axis_index("vn")
    row_energy = lax.dynamic_slice_in_dim(virt_energy, my_vw * tile_rows, tile_rows)
    energy_grid = virt_energy.reshape(n_vw, n_occ, sub_rows)
    col_energy = lax.dynamic_index_in_dim(energy_grid, my_occ, 1, keepdims=False).reshape(
        n_vw * sub_rows
    )
    share = n_vw * sub_rows // n_vn
    col_share = lax.dynamic_slice_in_dim(col_energy, my_vn * share, share)
    pieces = lax.all_to_all(slabs, "occ", split_axis=1, concat_axis=0, tiled=True)
    density = 0.0
    for index in range(pair_list.shape[0]):
        first = pair_list[index, 0]
        second = pair_list[index, 1]
        first_piece = lax.dynamic_index_in_dim(pieces, first, 0, keepdims=False)
        row_tile = lax.all_gather(first_piece, "occ", axis=0, tiled=True)
        col_piece = lax.dynamic_index_in_dim(pieces, second, 0, keepdims=False)
        integrals = contract_rows(row_tile, lax.all_gather(col_piece, "vw", axis=0, tiled=True))
        summed = lax.psum(integrals, "vn")
        mine = lax.dynamic_slice_in_dim(summed, my_vn * share, share, 1)
        denom = occ_energy[first] + occ_energy[second] - row_energy[:, None] - col_share[None, :]
        amplitude = (mine / denom).astype(jnp.bfloat16)
        density += contract_rows(amplitude, lax.all_gather(amplitude, "vw", axis=0, tiled=True))
    return lax.psum_scatter(density, ("occ", "vn"), scatter_dimension=1, tiled=True)


def grid_blocks(slabs, pair_list, occ_energy, virt_energy):
    n_vw, n_occ, n_vn = (lax.axis_size(name) for name in ("vw", "occ", "vn"))
    side = math.isqrt(n_occ * n_vn)
    depth = n_vw // (side * side)
    group = side // n_vn
    held, tile, k_dev = slabs.shape
    sub = tile // n_occ
    k_part = k_dev // n_occ
    x, w, v = (lax.axis_index(name) for name in ("occ", "vw", "vn"))
    r, s, y = w // (side * depth), w // depth % side, w % depth

    def at(row, col, deep):
        return (row % side * side + col % side) * depth + deep % depth

    places = [(a, b, c) for a in range(side) for b in range(side) for c in range(depth)]

    def send_vw(array, target):
        pairs = [(at(*place), at(*target(*place))) for place in places]
        if all(source == goal for source, goal in pairs):
            return array
        return lax.ppermute(array, "vw", pairs)

    def send_on(array, axis, extent, step):
        return lax.ppermute(array, axis, [(a, (a + step) % extent) for a in range(extent)])

    rows_by_sub = slabs.reshape(held, n_occ, sub, k_dev)
    energy = virt_energy.reshape(n_vw, n_occ, sub)
    chunks = cuts(sub, SHARES)

    lane_x, lane_a, lane_c, lane_y = Lane(LAG_X), Lane(LAG_Z), Lane(LAG_Z), Lane(LAG_Y)

    shares = []
    for low, high in chunks:
        rows = rows_by_sub[:, :, low:high]
        parts = [
            lax.dynamic_slice_in_dim(rows, (x + step) % n_occ * k_part, k_part, 3)
            for step in range(n_occ)
        ]
        shares.append(
            [parts[0]]
            + [
                Lane.send([lane_x], parts[step], lambda t, step=step: send_on(t, "occ", n_occ, step))
                for step in range(1, n_occ)
            ]
        )

    def orbital_rows(share, orbital):
        mine = [lax.dynamic_index_in_dim(part, orbital % held, 0, keepdims=False) for part in share]
        return pick(mine, (x - orbital // held) % n_occ)

    total = 0.0
    for index in range(pair_list.shape[0]):
        first, second = pair_list[index, 0], pair_list[index, 1]
        row_shares = [orbital_rows(share, first) for share in shares]
        col_shares = [
            jnp.roll(orbital_rows(share, second), -x, 0) for share in shares
        ]
        row_parts = [[part] + [None] * (side - 1) for part in row_shares]
        columns = [[None] * len(chunks) for _ in range(side)]

        def send_rows(h):
            for d in range(1, side):
                row_parts[h][d] = Lane.send(
                    [lane_a], row_shares[h], lambda t: send_vw(t, lambda a, b, c: (a, b - d, c))
                )

        def send_cols(d, h):
            lanes = [lane_c] if d == 0 else [lane_a, lane_c]
            arrived = Lane.send(
                lanes, col_shares[h], lambda t: send_vw(t, lambda a, b, c: (b - d, a, c))
            )
            columns[d][h] = [arrived] + [
                Lane.send([lane_y], arrived, lambda t: send_vw(t, lambda a, b, c: (a, b, c - l)))
                for l in range(1, depth)
            ]

        for h in range(len(chunks)):
            send_rows(h)
            send_cols(0, h)
        for d in range(1, side):
            for h in range(len(chunks)):
                send_cols(d, h)

        tiles = [
            jnp.concatenate([part[d] for part in row_parts], 1).reshape(tile, k_part)
            for d in range(side)
        ]
        row_sets = []
        for step in range(n_vn):
            core = (v + step) % n_vn
            row_sets.append(
                jnp.concatenate(
                    [pick(tiles, (q * n_vn + core - s) % side) for q in range(group)], 0
                )
            )
        row_index = [at(r, q * n_vn + v, y) for q in range(group)]
        row_energy = jnp.concatenate(
            [lax.dynamic_index_in_dim(energy, i, 0, keepdims=False).reshape(tile) for i in row_index]
        )
        pair_energy = occ_energy[first] + occ_energy[second]

        amplitude = []
        for d in range(side):
            blocks = []
            begin = 0
            for end in ends_of(FIRST_SETS if d == 0 else OTHER_SETS, len(chunks)):
                low, high = chunks[begin][0], chunks[end - 1][1]
                these = jnp.concatenate(
                    [
                        jnp.stack([columns[d][h][l] for l in range(depth)], 1)
                        for h in range(begin, end)
                    ],
                    2,
                ).reshape(n_occ * depth * (high - low), k_part)
                begin = end
                partial = [contract_rows(these, rows) for rows in row_sets]
                kept = partial[0]
                for step in range(1, n_vn):
                    kept = kept + send_on(partial[step], "vn", n_vn, step)
                kept = kept.reshape(n_occ, depth * (high - low), kept.shape[1])
                integrals = kept[0]
                for step in range(1, n_occ):
                    integrals = integrals + Lane.send(
                        [lane_x],
                        kept[step].astype(TERM),
                        lambda t, step=step: send_on(t, "occ", n_occ, step),
                    ).astype(jnp.float32)
                col_energy = jnp.concatenate(
                    [
                        lax.dynamic_slice(
                            energy, (at(s, r + d, y + l), x, low), (1, 1, high - low)
                        ).reshape(high - low)
                        for l in range(depth)
                    ]
                )
                denom = pair_energy - row_energy[None, :] - col_energy[:, None]
                block = (integrals / denom).astype(jnp.bfloat16)
                blocks.append(block.reshape(depth, high - low, block.shape[1]))
            amplitude.append(jnp.concatenate(blocks, 1))

        width = group * tile
        halves = cuts(tile, HALVES, 128)
        gathered = [[[None] * side for _ in range(depth)] for _ in range(side)]

        def part_of(array, low, high):
            parts = [array[:, :, q * tile + low : q * tile + high] for q in range(group)]
            return parts[0] if group == 1 else jnp.concatenate(parts, 2)

        def over_y(c):
            return lambda t: send_vw(t, lambda i, j, k: (i, j, k - c))

        def over_r(a):
            return lambda t: send_vw(t, lambda i, j, k: (i - a, j, k))

        for d in range(side):
            mine = amplitude[d]
            gathered[0][0][d] = [part_of(mine, low, high) for low, high in halves]
            split = halves if d == side - 1 else [(0, tile)]
            for a in range(1, side):
                gathered[a][0][d] = [
                    Lane.send([lane_a, lane_c], part_of(mine, low, high), over_r(a))
                    for low, high in split
                ]
            for c in range(1, depth):
                arrived = Lane.send([lane_y], mine, over_y(c))
                gathered[0][c][d] = [part_of(arrived, low, high) for low, high in halves]
        for d in range(side):
            for a in range(1, side):
                for c in range(1, depth):
                    gathered[a][c][d] = [
                        Lane.send([lane_y], part, over_y(c)) for part in gathered[a][0][d]
                    ]
                for c in range(depth):
                    if len(gathered[a][c][d]) < len(halves):
                        gathered[a][c][d] = [
                            part_of(gathered[a][c][d][0], low, high) for low, high in halves
                        ]

        mine = jnp.stack(amplitude).reshape(side * depth * sub, width)
        cores = [mine] + [
            send_on(mine, "vn", n_vn, n_vn - step) for step in range(1, n_vn)
        ]
        count = mine.shape[0]
        by_s = [
            pick([core.reshape(count, group, tile)[:, q] for core in cores], (b - v) % n_vn)
            for q in range(group)
            for b in range(n_vn)
        ]
        left = [pick(by_s, (s + d) % side) for d in range(side)]

        def arranged(a, c, part):
            return jnp.concatenate(
                [
                    gathered[a][c][(d - a) % side][part][(l - c) % depth]
                    for d in range(side)
                    for l in range(depth)
                ],
                0,
            )

        def move_on(array, lane, move):
            return Lane.send([lane], array.astype(jnp.bfloat16), move).astype(jnp.float32)

        def over_occ(step):
            return lambda t: send_on(t, "occ", n_occ, step)

        def over_s(d):
            return lambda t: send_vw(t, lambda i, j, k: (i, j + d, k))

        kept = {}

        def rights_of(part, c):
            options = [arranged(a, c, part) for a in range(side)]
            if group > 1:
                size = options[0].shape[1] // group
                options = [o[:, q * size : (q + 1) * size] for o in options for q in range(group)]
            chosen = []
            for step in range(n_occ):
                goal = (x + step) % n_occ
                chosen.append(pick(options, (goal // group - r) % side * group + goal % group))
            return chosen

        def occ_first(part, c):
            rights = rights_of(part, c)
            every = jnp.concatenate(left, 1)
            here = contract_first(every, rights[0])
            for step in range(1, n_occ):
                here = here + move_on(contract_first(every, rights[step]), lane_x, over_occ(step))
            kept[part, c] = here.reshape(side, tile, here.shape[1])

        def s_second(part, c):
            here = kept[part, c][0]
            for d in range(1, side):
                here = here + move_on(kept[part, c][d], lane_a, over_s(d))
            kept[part, c] = here

        def s_first(part, c):
            every = jnp.concatenate(rights_of(part, c), 1)
            here = contract_first(left[0], every)
            for d in range(1, side):
                here = here + move_on(contract_first(left[d], every), lane_a, over_s(d))
            kept[part, c] = here

        def occ_second(part, c):
            size = kept[part, c].shape[1] // n_occ
            here = kept[part, c][:, :size]
            for step in range(1, n_occ):
                here = here + move_on(
                    kept[part, c][:, step * size : (step + 1) * size], lane_x, over_occ(step)
                )
            kept[part, c] = here

        even, odd = range(0, depth, 2), range(1, depth, 2)
        for part in range(len(halves) + 1):
            if part < len(halves):
                for c in even:
                    occ_first(part, c)
            if part > 0:
                for c in odd:
                    occ_second(part - 1, c)
            if part < len(halves):
                for c in odd:
                    s_first(part, c)
                for c in even:
                    s_second(part, c)
        found = [[kept[part, c] for part in range(len(halves))] for c in range(depth)]
        whole = [jnp.concatenate(parts, 1) for parts in found]
        total = total + jnp.concatenate([pick(whole, (c - y) % depth) for c in range(depth)], 1)
    return total


def solution(mesh):
    in_specs = (P("occ", "vw", "vn"), P(), P(), P())
    out_specs = P("vw", ("occ", "vn"))
    n_occ, n_vw, n_vn = (mesh.shape[name] for name in ("occ", "vw", "vn"))
    side = math.isqrt(n_occ * n_vn)
    fits = side * side == n_occ * n_vn and n_vw % (side * side) == 0 and side % n_vn == 0
    return jax.shard_map(
        grid_blocks if fits else whole_rows,
        mesh=mesh,
        in_specs=in_specs,
        out_specs=out_specs,
        check_vma=False,
    )
```

```python
import math

import jax
import jax.numpy as jnp
from jax import lax
from jax.sharding import PartitionSpec as P

SHARES = (1, 1, 1, 1)
FIRST_SETS = (2, 4)
OTHER_SETS = (2, 3, 4)
HALVES = (3, 2)
TERM = jnp.float32
LATE = jnp.bfloat16
LAG_X = 9
LAG_Z = 1
LAG_Y = 1


def contract_rows(left, piece):
    return lax.dot_general(
        left, piece, (((1,), (1,)), ((), ())), preferred_element_type=jnp.float32
    )


def contract_first(left, right):
    return lax.dot_general(
        left, right, (((0,), (0,)), ((), ())), preferred_element_type=jnp.float32
    )


def pick(items, index):
    chosen = items[0]
    for position in range(1, len(items)):
        chosen = jnp.where(index == position, items[position], chosen)
    return chosen


def cuts(extent, shares, unit=16):
    whole = sum(shares)
    if extent % unit or extent // unit < whole:
        unit = 1
    marks = [extent // unit * sum(shares[:part]) // whole * unit for part in range(len(shares) + 1)]
    return [(low, high) for low, high in zip(marks, marks[1:]) if high > low]


def ends_of(sets, count):
    return sorted({min(end, count) for end in sets} | {count})


class Lane:
    def __init__(self, lag):
        self.arrived = []
        self.lag = lag

    @staticmethod
    def send(lanes, array, move):
        waits = [lane.arrived[-lane.lag] for lane in lanes if len(lane.arrived) >= lane.lag]
        if waits:
            array, *_ = lax.optimization_barrier((array, *waits))
        result = move(array)
        for lane in lanes:
            lane.arrived.append(result)
        return result


def whole_rows(slabs, pair_list, occ_energy, virt_energy):
    n_vw = lax.axis_size("vw")
    n_occ = lax.axis_size("occ")
    n_vn = lax.axis_size("vn")
    tile_rows = slabs.shape[1]
    sub_rows = tile_rows // n_occ
    my_occ = lax.axis_index("occ")
    my_vw = lax.axis_index("vw")
    my_vn = lax.axis_index("vn")
    row_energy = lax.dynamic_slice_in_dim(virt_energy, my_vw * tile_rows, tile_rows)
    energy_grid = virt_energy.reshape(n_vw, n_occ, sub_rows)
    col_energy = lax.dynamic_index_in_dim(energy_grid, my_occ, 1, keepdims=False).reshape(
        n_vw * sub_rows
    )
    share = n_vw * sub_rows // n_vn
    col_share = lax.dynamic_slice_in_dim(col_energy, my_vn * share, share)
    pieces = lax.all_to_all(slabs, "occ", split_axis=1, concat_axis=0, tiled=True)
    density = 0.0
    for index in range(pair_list.shape[0]):
        first = pair_list[index, 0]
        second = pair_list[index, 1]
        first_piece = lax.dynamic_index_in_dim(pieces, first, 0, keepdims=False)
        row_tile = lax.all_gather(first_piece, "occ", axis=0, tiled=True)
        col_piece = lax.dynamic_index_in_dim(pieces, second, 0, keepdims=False)
        integrals = contract_rows(row_tile, lax.all_gather(col_piece, "vw", axis=0, tiled=True))
        summed = lax.psum(integrals, "vn")
        mine = lax.dynamic_slice_in_dim(summed, my_vn * share, share, 1)
        denom = occ_energy[first] + occ_energy[second] - row_energy[:, None] - col_share[None, :]
        amplitude = (mine / denom).astype(jnp.bfloat16)
        density += contract_rows(amplitude, lax.all_gather(amplitude, "vw", axis=0, tiled=True))
    return lax.psum_scatter(density, ("occ", "vn"), scatter_dimension=1, tiled=True)


def grid_blocks(slabs, pair_list, occ_energy, virt_energy):
    n_vw, n_occ, n_vn = (lax.axis_size(name) for name in ("vw", "occ", "vn"))
    side = math.isqrt(n_occ * n_vn)
    depth = n_vw // (side * side)
    group = side // n_vn
    held, tile, k_dev = slabs.shape
    sub = tile // n_occ
    k_part = k_dev // n_occ
    x, w, v = (lax.axis_index(name) for name in ("occ", "vw", "vn"))
    r, s, y = w // (side * depth), w // depth % side, w % depth

    def at(row, col, deep):
        return (row % side * side + col % side) * depth + deep % depth

    places = [(a, b, c) for a in range(side) for b in range(side) for c in range(depth)]

    def send_vw(array, target):
        pairs = [(at(*place), at(*target(*place))) for place in places]
        if all(source == goal for source, goal in pairs):
            return array
        return lax.ppermute(array, "vw", pairs)

    def send_on(array, axis, extent, step):
        return lax.ppermute(array, axis, [(a, (a + step) % extent) for a in range(extent)])

    rows_by_sub = slabs.reshape(held, n_occ, sub, k_dev)
    energy = virt_energy.reshape(n_vw, n_occ, sub)
    chunks = cuts(sub, SHARES)

    lane_x, lane_a, lane_c, lane_y = Lane(LAG_X), Lane(LAG_Z), Lane(LAG_Z), Lane(LAG_Y)

    shares = []
    for low, high in chunks:
        rows = rows_by_sub[:, :, low:high]
        parts = [
            lax.dynamic_slice_in_dim(rows, (x + step) % n_occ * k_part, k_part, 3)
            for step in range(n_occ)
        ]
        shares.append(
            [parts[0]]
            + [
                Lane.send([lane_x], parts[step], lambda t, step=step: send_on(t, "occ", n_occ, step))
                for step in range(1, n_occ)
            ]
        )

    def orbital_rows(share, orbital):
        mine = [lax.dynamic_index_in_dim(part, orbital % held, 0, keepdims=False) for part in share]
        return pick(mine, (x - orbital // held) % n_occ)

    total = 0.0
    for index in range(pair_list.shape[0]):
        first, second = pair_list[index, 0], pair_list[index, 1]
        row_shares = [orbital_rows(share, first) for share in shares]
        col_shares = [
            jnp.roll(orbital_rows(share, second), -x, 0) for share in shares
        ]
        row_parts = [[part] + [None] * (side - 1) for part in row_shares]
        columns = [[None] * len(chunks) for _ in range(side)]

        def send_rows(h):
            for d in range(1, side):
                row_parts[h][d] = Lane.send(
                    [lane_a], row_shares[h], lambda t: send_vw(t, lambda a, b, c: (a, b - d, c))
                )

        def send_cols(d, h):
            lanes = [lane_c] if d == 0 else [lane_a, lane_c]
            arrived = Lane.send(
                lanes, col_shares[h], lambda t: send_vw(t, lambda a, b, c: (b - d, a, c))
            )
            columns[d][h] = [arrived] + [
                Lane.send([lane_y], arrived, lambda t: send_vw(t, lambda a, b, c: (a, b, c - l)))
                for l in range(1, depth)
            ]

        for h in range(len(chunks)):
            send_rows(h)
            send_cols(0, h)
        for d in range(1, side):
            for h in range(len(chunks)):
                send_cols(d, h)

        tiles = [
            jnp.concatenate([part[d] for part in row_parts], 1).reshape(tile, k_part)
            for d in range(side)
        ]
        row_sets = []
        for step in range(n_vn):
            core = (v + step) % n_vn
            row_sets.append(
                jnp.concatenate(
                    [pick(tiles, (q * n_vn + core - s) % side) for q in range(group)], 0
                )
            )
        row_index = [at(r, q * n_vn + v, y) for q in range(group)]
        row_energy = jnp.concatenate(
            [lax.dynamic_index_in_dim(energy, i, 0, keepdims=False).reshape(tile) for i in row_index]
        )
        pair_energy = occ_energy[first] + occ_energy[second]

        amplitude = []
        for d in range(side):
            blocks = []
            begin = 0
            for end in ends_of(FIRST_SETS if d == 0 else OTHER_SETS, len(chunks)):
                low, high = chunks[begin][0], chunks[end - 1][1]
                these = jnp.concatenate(
                    [
                        jnp.stack([columns[d][h][l] for l in range(depth)], 1)
                        for h in range(begin, end)
                    ],
                    2,
                ).reshape(n_occ * depth * (high - low), k_part)
                begin = end
                partial = [contract_rows(these, rows) for rows in row_sets]
                kept = partial[0]
                for step in range(1, n_vn):
                    kept = kept + send_on(partial[step], "vn", n_vn, step)
                kept = kept.reshape(n_occ, depth * (high - low), kept.shape[1])
                integrals = kept[0]
                for step in range(1, n_occ):
                    integrals = integrals + Lane.send(
                        [lane_x],
                        kept[step].astype(TERM if d == 0 else LATE),
                        lambda t, step=step: send_on(t, "occ", n_occ, step),
                    ).astype(jnp.float32)
                col_energy = jnp.concatenate(
                    [
                        lax.dynamic_slice(
                            energy, (at(s, r + d, y + l), x, low), (1, 1, high - low)
                        ).reshape(high - low)
                        for l in range(depth)
                    ]
                )
                denom = pair_energy - row_energy[None, :] - col_energy[:, None]
                block = (integrals / denom).astype(jnp.bfloat16)
                blocks.append(block.reshape(depth, high - low, block.shape[1]))
            amplitude.append(jnp.concatenate(blocks, 1))

        width = group * tile
        halves = cuts(tile, HALVES, 128)
        gathered = [[[None] * side for _ in range(depth)] for _ in range(side)]

        def part_of(array, low, high):
            parts = [array[:, :, q * tile + low : q * tile + high] for q in range(group)]
            return parts[0] if group == 1 else jnp.concatenate(parts, 2)

        def over_y(c):
            return lambda t: send_vw(t, lambda i, j, k: (i, j, k - c))

        def over_r(a):
            return lambda t: send_vw(t, lambda i, j, k: (i - a, j, k))

        for d in range(side):
            mine = amplitude[d]
            gathered[0][0][d] = [part_of(mine, low, high) for low, high in halves]
            split = halves if d == side - 1 else [(0, tile)]
            for a in range(1, side):
                gathered[a][0][d] = [
                    Lane.send([lane_a, lane_c], part_of(mine, low, high), over_r(a))
                    for low, high in split
                ]
            for c in range(1, depth):
                arrived = Lane.send([lane_y], mine, over_y(c))
                gathered[0][c][d] = [part_of(arrived, low, high) for low, high in halves]
        for d in range(side):
            for a in range(1, side):
                for c in range(1, depth):
                    gathered[a][c][d] = [
                        Lane.send([lane_y], part, over_y(c)) for part in gathered[a][0][d]
                    ]
                for c in range(depth):
                    if len(gathered[a][c][d]) < len(halves):
                        gathered[a][c][d] = [
                            part_of(gathered[a][c][d][0], low, high) for low, high in halves
                        ]

        mine = jnp.stack(amplitude).reshape(side * depth * sub, width)
        cores = [mine] + [
            send_on(mine, "vn", n_vn, n_vn - step) for step in range(1, n_vn)
        ]
        count = mine.shape[0]
        by_s = [
            pick([core.reshape(count, group, tile)[:, q] for core in cores], (b - v) % n_vn)
            for q in range(group)
            for b in range(n_vn)
        ]
        left = [pick(by_s, (s + d) % side) for d in range(side)]

        def arranged(a, c, part):
            return jnp.concatenate(
                [
                    gathered[a][c][(d - a) % side][part][(l - c) % depth]
                    for d in range(side)
                    for l in range(depth)
                ],
                0,
            )

        def move_on(array, lane, move):
            return Lane.send([lane], array.astype(jnp.bfloat16), move).astype(jnp.float32)

        def over_occ(step):
            return lambda t: send_on(t, "occ", n_occ, step)

        def over_s(d):
            return lambda t: send_vw(t, lambda i, j, k: (i, j + d, k))

        kept = {}

        def rights_of(part, c):
            options = [arranged(a, c, part) for a in range(side)]
            if group > 1:
                size = options[0].shape[1] // group
                options = [o[:, q * size : (q + 1) * size] for o in options for q in range(group)]
            chosen = []
            for step in range(n_occ):
                goal = (x + step) % n_occ
                chosen.append(pick(options, (goal // group - r) % side * group + goal % group))
            return chosen

        def occ_first(part, c):
            rights = rights_of(part, c)
            every = jnp.concatenate(left, 1)
            here = contract_first(every, rights[0])
            for step in range(1, n_occ):
                here = here + move_on(contract_first(every, rights[step]), lane_x, over_occ(step))
            kept[part, c] = here.reshape(side, tile, here.shape[1])

        def s_second(part, c):
            here = kept[part, c][0]
            for d in range(1, side):
                here = here + move_on(kept[part, c][d], lane_a, over_s(d))
            kept[part, c] = here

        def s_first(part, c):
            every = jnp.concatenate(rights_of(part, c), 1)
            here = contract_first(left[0], every)
            for d in range(1, side):
                here = here + move_on(contract_first(left[d], every), lane_a, over_s(d))
            kept[part, c] = here

        def occ_second(part, c):
            size = kept[part, c].shape[1] // n_occ
            here = kept[part, c][:, :size]
            for step in range(1, n_occ):
                here = here + move_on(
                    kept[part, c][:, step * size : (step + 1) * size], lane_x, over_occ(step)
                )
            kept[part, c] = here

        even, odd = range(0, depth, 2), range(1, depth, 2)
        for part in range(len(halves) + 1):
            if part < len(halves):
                for c in even:
                    occ_first(part, c)
            if part > 0:
                for c in odd:
                    occ_second(part - 1, c)
            if part < len(halves):
                for c in odd:
                    s_first(part, c)
                for c in even:
                    s_second(part, c)
        found = [[kept[part, c] for part in range(len(halves))] for c in range(depth)]
        whole = [jnp.concatenate(parts, 1) for parts in found]
        total = total + jnp.concatenate([pick(whole, (c - y) % depth) for c in range(depth)], 1)
    return total


def solution(mesh):
    in_specs = (P("occ", "vw", "vn"), P(), P(), P())
    out_specs = P("vw", ("occ", "vn"))
    n_occ, n_vw, n_vn = (mesh.shape[name] for name in ("occ", "vw", "vn"))
    side = math.isqrt(n_occ * n_vn)
    fits = side * side == n_occ * n_vn and n_vw % (side * side) == 0 and side % n_vn == 0
    return jax.shard_map(
        grid_blocks if fits else whole_rows,
        mesh=mesh,
        in_specs=in_specs,
        out_specs=out_specs,
        check_vma=False,
    )
```

```python
import math

import jax
import jax.numpy as jnp
from jax import lax
from jax.sharding import PartitionSpec as P

SHARES = (1, 1, 1, 1)
FIRST_SETS = (2, 4)
OTHER_SETS = (2, 3, 4)
HALVES = (3, 2)
TERM = jnp.bfloat16
TIE = False
WHOLE = False
READY = False
SIMPLE = False
LAG_X = 9
APART = False
LAG_Z = 1
LAG_Y = 1


def contract_rows(left, piece):
    return lax.dot_general(
        left, piece, (((1,), (1,)), ((), ())), preferred_element_type=jnp.float32
    )


def contract_first(left, right):
    return lax.dot_general(
        left, right, (((0,), (0,)), ((), ())), preferred_element_type=jnp.float32
    )


def pick(items, index):
    chosen = items[0]
    for position in range(1, len(items)):
        chosen = jnp.where(index == position, items[position], chosen)
    return chosen


def cuts(extent, shares, unit=16):
    whole = sum(shares)
    if extent % unit or extent // unit < whole:
        unit = 1
    marks = [extent // unit * sum(shares[:part]) // whole * unit for part in range(len(shares) + 1)]
    return [(low, high) for low, high in zip(marks, marks[1:]) if high > low]


def ends_of(sets, count):
    return sorted({min(end, count) for end in sets} | {count})


class Lane:
    def __init__(self, lag):
        self.arrived = []
        self.lag = lag

    @staticmethod
    def send(lanes, array, move):
        waits = [lane.arrived[-lane.lag] for lane in lanes if len(lane.arrived) >= lane.lag]
        if waits:
            array, *_ = lax.optimization_barrier((array, *waits))
        result = move(array)
        for lane in lanes:
            lane.arrived.append(result)
        return result


def whole_rows(slabs, pair_list, occ_energy, virt_energy):
    n_vw = lax.axis_size("vw")
    n_occ = lax.axis_size("occ")
    n_vn = lax.axis_size("vn")
    tile_rows = slabs.shape[1]
    sub_rows = tile_rows // n_occ
    my_occ = lax.axis_index("occ")
    my_vw = lax.axis_index("vw")
    my_vn = lax.axis_index("vn")
    row_energy = lax.dynamic_slice_in_dim(virt_energy, my_vw * tile_rows, tile_rows)
    energy_grid = virt_energy.reshape(n_vw, n_occ, sub_rows)
    col_energy = lax.dynamic_index_in_dim(energy_grid, my_occ, 1, keepdims=False).reshape(
        n_vw * sub_rows
    )
    share = n_vw * sub_rows // n_vn
    col_share = lax.dynamic_slice_in_dim(col_energy, my_vn * share, share)
    pieces = lax.all_to_all(slabs, "occ", split_axis=1, concat_axis=0, tiled=True)
    density = 0.0
    for index in range(pair_list.shape[0]):
        first = pair_list[index, 0]
        second = pair_list[index, 1]
        first_piece = lax.dynamic_index_in_dim(pieces, first, 0, keepdims=False)
        row_tile = lax.all_gather(first_piece, "occ", axis=0, tiled=True)
        col_piece = lax.dynamic_index_in_dim(pieces, second, 0, keepdims=False)
        integrals = contract_rows(row_tile, lax.all_gather(col_piece, "vw", axis=0, tiled=True))
        summed = lax.psum(integrals, "vn")
        mine = lax.dynamic_slice_in_dim(summed, my_vn * share, share, 1)
        denom = occ_energy[first] + occ_energy[second] - row_energy[:, None] - col_share[None, :]
        amplitude = (mine / denom).astype(jnp.bfloat16)
        density += contract_rows(amplitude, lax.all_gather(amplitude, "vw", axis=0, tiled=True))
    return lax.psum_scatter(density, ("occ", "vn"), scatter_dimension=1, tiled=True)


def grid_blocks(slabs, pair_list, occ_energy, virt_energy):
    n_vw, n_occ, n_vn = (lax.axis_size(name) for name in ("vw", "occ", "vn"))
    side = math.isqrt(n_occ * n_vn)
    depth = n_vw // (side * side)
    group = side // n_vn
    held, tile, k_dev = slabs.shape
    sub = tile // n_occ
    k_part = k_dev // n_occ
    x, w, v = (lax.axis_index(name) for name in ("occ", "vw", "vn"))
    r, s, y = w // (side * depth), w // depth % side, w % depth

    def at(row, col, deep):
        return (row % side * side + col % side) * depth + deep % depth

    places = [(a, b, c) for a in range(side) for b in range(side) for c in range(depth)]

    def send_vw(array, target):
        pairs = [(at(*place), at(*target(*place))) for place in places]
        if all(source == goal for source, goal in pairs):
            return array
        return lax.ppermute(array, "vw", pairs)

    def send_on(array, axis, extent, step):
        return lax.ppermute(array, axis, [(a, (a + step) % extent) for a in range(extent)])

    rows_by_sub = slabs.reshape(held, n_occ, sub, k_dev)
    energy = virt_energy.reshape(n_vw, n_occ, sub)
    chunks = cuts(sub, SHARES)

    lane_x, lane_a, lane_c, lane_y = Lane(LAG_X), Lane(LAG_Z), Lane(LAG_Z), Lane(LAG_Y)

    shares = []
    for low, high in chunks:
        rows = lax.optimization_barrier(rows_by_sub[:, :, low:high]) if APART else rows_by_sub[:, :, low:high]
        parts = [
            lax.dynamic_slice_in_dim(rows, (x + step) % n_occ * k_part, k_part, 3)
            for step in range(n_occ)
        ]
        shares.append(
            [parts[0]]
            + [
                Lane.send([lane_x], parts[step], lambda t, step=step: send_on(t, "occ", n_occ, step))
                for step in range(1, n_occ)
            ]
        )

    def orbital_rows(share, orbital):
        mine = [lax.dynamic_index_in_dim(part, orbital % held, 0, keepdims=False) for part in share]
        return pick(mine, (x - orbital // held) % n_occ)

    total = 0.0
    for index in range(pair_list.shape[0]):
        first, second = pair_list[index, 0], pair_list[index, 1]
        row_shares = [orbital_rows(share, first) for share in shares]
        col_shares = [
            jnp.roll(orbital_rows(share, second), -x, 0) for share in shares
        ]
        row_parts = [[part] + [None] * (side - 1) for part in row_shares]
        columns = [[None] * len(chunks) for _ in range(side)]

        def send_rows(h):
            for d in range(1, side):
                row_parts[h][d] = Lane.send(
                    [lane_a], row_shares[h], lambda t: send_vw(t, lambda a, b, c: (a, b - d, c))
                )

        def send_cols(d, h, after=None):
            lanes = [lane_c] if d == 0 else [lane_a, lane_c]
            arrived = Lane.send(lanes, col_shares[h], lambda t: send_vw(t, lambda a, b, c: (b - d, a, c)))
            if after is not None:
                arrived, _ = lax.optimization_barrier((arrived, after))
            columns[d][h] = [arrived] + [
                Lane.send([lane_y], arrived, lambda t: send_vw(t, lambda a, b, c: (a, b, c - l)))
                for l in range(1, depth)
            ]

        for h in range(len(chunks)):
            send_rows(h)
            send_cols(0, h)

        tiles = [
            jnp.concatenate([part[d] for part in row_parts], 1).reshape(tile, k_part)
            for d in range(side)
        ]
        row_sets = []
        for step in range(n_vn):
            core = (v + step) % n_vn
            row_sets.append(
                jnp.concatenate(
                    [pick(tiles, (q * n_vn + core - s) % side) for q in range(group)], 0
                )
            )
        row_index = [at(r, q * n_vn + v, y) for q in range(group)]
        row_energy = jnp.concatenate(
            [lax.dynamic_index_in_dim(energy, i, 0, keepdims=False).reshape(tile) for i in row_index]
        )
        pair_energy = occ_energy[first] + occ_energy[second]

        def integral_terms(d, begin, end):
            these = jnp.concatenate(
                [
                    jnp.stack([columns[d][h][l] for l in range(depth)], 1)
                    for h in range(begin, end)
                ],
                2,
            )
            these = these.reshape(-1, k_part)
            if SIMPLE:
                these = lax.optimization_barrier(these)
            partial = [contract_rows(these, rows) for rows in row_sets]
            kept = partial[0]
            for step in range(1, n_vn):
                kept = kept + send_on(partial[step], "vn", n_vn, step)
            return kept.reshape(n_occ, -1, kept.shape[1])

        def amplitudes(d, begin, end, kept):
            low, high = chunks[begin][0], chunks[end - 1][1]
            integrals = kept[0]
            for step in range(1, n_occ):
                arrived = Lane.send(
                    [lane_x],
                    kept[step].astype(TERM),
                    lambda t: send_on(t, "occ", n_occ, step),
                )
                integrals = integrals + arrived.astype(jnp.float32)
            col_energy = jnp.concatenate(
                [
                    lax.dynamic_slice(
                        energy, (at(s, r + d, y + l), x, low), (1, 1, high - low)
                    ).reshape(high - low)
                    for l in range(depth)
                ]
            )
            denom = pair_energy - row_energy[None, :] - col_energy[:, None]
            block = (integrals / denom).astype(jnp.bfloat16)
            return block.reshape(depth, high - low, block.shape[1])

        width = group * tile
        halves = cuts(tile, HALVES, 128)
        amplitude = [None] * side
        gathered = [[[None] * side for _ in range(depth)] for _ in range(side)]

        def part_of(array, low, high):
            parts = [array[:, :, q * tile + low : q * tile + high] for q in range(group)]
            return parts[0] if group == 1 else jnp.concatenate(parts, 2)

        def over_y(c):
            return lambda t: send_vw(t, lambda i, j, k: (i, j, k - c))

        def over_r(a):
            return lambda t: send_vw(t, lambda i, j, k: (i - a, j, k))

        def gather_r(d):
            mine = amplitude[d]
            gathered[0][0][d] = [part_of(mine, low, high) for low, high in halves]
            for a in range(1, side):
                gathered[a][0][d] = [
                    Lane.send([lane_a, lane_c], part_of(mine, low, high), over_r(a))
                    for low, high in ([(0, tile)] if WHOLE and d < side - 1 else halves)
                ]

        waiting = []
        blocks = []
        begin = 0
        for end in ends_of(FIRST_SETS, len(chunks)):
            kept = integral_terms(0, begin, end)
            waiting.append(kept)
            blocks.append(amplitudes(0, begin, end, kept))
            begin = end
        amplitude[0] = jnp.concatenate(blocks, 1)
        for d in range(1, side):
            begin = 0
            blocks = []
            ends = ends_of(OTHER_SETS, len(chunks))
            for h in range(len(chunks)):
                send_cols(d, h, waiting.pop(0) if READY and h >= READY and waiting else None)
                if h + 1 == len(chunks):
                    gather_r(d - 1)
                    if TIE:
                        columns[d][h][-1], *_ = lax.optimization_barrier(
                            (columns[d][h][-1], gathered[1][0][d - 1][0])
                        )
                if h + 1 in ends:
                    kept = integral_terms(d, begin, h + 1)
                    blocks.append(amplitudes(d, begin, h + 1, kept))
                    begin = h + 1
            amplitude[d] = jnp.concatenate(blocks, 1)
        gather_r(side - 1)
        for d in range(side):
            for c in range(1, depth):
                arrived = Lane.send([lane_y], amplitude[d], over_y(c))
                gathered[0][c][d] = [part_of(arrived, low, high) for low, high in halves]
        for d in range(side):
            for a in range(1, side):
                for c in range(1, depth):
                    if d < side - 1:
                        arrived = gathered[a][0][d]
                        arrived = arrived[0] if len(arrived) == 1 else jnp.concatenate(arrived, 2)
                        arrived = Lane.send([lane_y], arrived, over_y(c))
                        marks = [0]
                        for low, high in halves:
                            marks.append(marks[-1] + group * (high - low))
                        gathered[a][c][d] = [
                            arrived[:, :, low:high] for low, high in zip(marks, marks[1:])
                        ]
                    else:
                        gathered[a][c][d] = [
                            Lane.send([lane_y], part, over_y(c)) for part in gathered[a][0][d]
                        ]

        for d in range(side - 1):
            for a in range(1, side):
                if len(gathered[a][0][d]) < len(halves):
                    gathered[a][0][d] = [
                        part_of(gathered[a][0][d][0], low, high) for low, high in halves
                    ]

        mine = jnp.stack(amplitude).reshape(side * depth * sub, width)
        cores = [mine] + [
            send_on(mine, "vn", n_vn, n_vn - step) for step in range(1, n_vn)
        ]
        count = mine.shape[0]
        by_s = [
            pick([core.reshape(count, group, tile)[:, q] for core in cores], (b - v) % n_vn)
            for q in range(group)
            for b in range(n_vn)
        ]
        left = [pick(by_s, (s + d) % side) for d in range(side)]

        def arranged(a, c, part):
            return jnp.concatenate(
                [
                    gathered[a][c][(d - a) % side][part][(l - c) % depth]
                    for d in range(side)
                    for l in range(depth)
                ],
                0,
            )

        def move_on(array, lane, move):
            return Lane.send([lane], array.astype(jnp.bfloat16), move).astype(jnp.float32)

        def over_occ(step):
            return lambda t: send_on(t, "occ", n_occ, step)

        def over_s(d):
            return lambda t: send_vw(t, lambda i, j, k: (i, j + d, k))

        kept = {}

        def rights_of(part, c):
            options = [arranged(a, c, part) for a in range(side)]
            if group > 1:
                size = options[0].shape[1] // group
                options = [o[:, q * size : (q + 1) * size] for o in options for q in range(group)]
            chosen = []
            for step in range(n_occ):
                goal = (x + step) % n_occ
                chosen.append(pick(options, (goal // group - r) % side * group + goal % group))
            return chosen

        def occ_first(part, c):
            rights = rights_of(part, c)
            every = jnp.concatenate(left, 1)
            here = contract_first(every, rights[0])
            for step in range(1, n_occ):
                here = here + move_on(contract_first(every, rights[step]), lane_x, over_occ(step))
            kept[part, c] = here.reshape(side, tile, here.shape[1])

        def s_second(part, c):
            here = kept[part, c][0]
            for d in range(1, side):
                here = here + move_on(kept[part, c][d], lane_a, over_s(d))
            kept[part, c] = here

        def s_first(part, c):
            every = jnp.concatenate(rights_of(part, c), 1)
            here = contract_first(left[0], every)
            for d in range(1, side):
                here = here + move_on(contract_first(left[d], every), lane_a, over_s(d))
            kept[part, c] = here

        def occ_second(part, c):
            size = kept[part, c].shape[1] // n_occ
            here = kept[part, c][:, :size]
            for step in range(1, n_occ):
                here = here + move_on(
                    kept[part, c][:, step * size : (step + 1) * size], lane_x, over_occ(step)
                )
            kept[part, c] = here

        even, odd = range(0, depth, 2), range(1, depth, 2)
        for part in range(len(halves) + 1):
            if part < len(halves):
                for c in even:
                    occ_first(part, c)
            if part > 0:
                for c in odd:
                    occ_second(part - 1, c)
            if part < len(halves):
                for c in odd:
                    s_first(part, c)
                for c in even:
                    s_second(part, c)
        found = [[kept[part, c] for part in range(len(halves))] for c in range(depth)]
        whole = [jnp.concatenate(parts, 1) for parts in found]
        total = total + jnp.concatenate([pick(whole, (c - y) % depth) for c in range(depth)], 1)
    return total


def solution(mesh):
    in_specs = (P("occ", "vw", "vn"), P(), P(), P())
    out_specs = P("vw", ("occ", "vn"))
    n_occ, n_vw, n_vn = (mesh.shape[name] for name in ("occ", "vw", "vn"))
    side = math.isqrt(n_occ * n_vn)
    fits = side * side == n_occ * n_vn and n_vw % (side * side) == 0 and side % n_vn == 0
    return jax.shard_map(
        grid_blocks if fits else whole_rows,
        mesh=mesh,
        in_specs=in_specs,
        out_specs=out_specs,
        check_vma=False,
    )
```
